32 devices in a mesh: rep: 2 (over y), row: 4 (over z), col: 4 (over x, core).
Axes of the slice: x: 2, y: 2, z: 4, core: 2. Of those that a mesh axis runs over, the one named last changes fastest.
Arguments:
- hidden_in: bfloat16 [8, 16384], P('rep', 'row'), parts along dimension 0, may hold values from -6 to 6
- norm_gain: float32 [16384], P('row'), may hold values from 0.5 to 1.5
- w_query: bfloat16 [16384, 8192], P('row', 'col'), may hold values from -0.046875 to 0.046875
- key_weight: bfloat16 [16384, 512], P('row', 'col'), may hold values from -0.046875 to 0.046875
- value_weight: bfloat16 [16384, 512], P('row', 'col'), may hold values from -0.046875 to 0.046875
- w_output: bfloat16 [8192, 16384], P('col', 'row'), may hold values from -3 to 3
- stored_keys: bfloat16 [8, 2048, 512], P(('rep', 'row'), None, 'col'), parts along dimension 0, may hold values from -480 to 480
- stored_values: bfloat16 [8, 2048, 512], P(('rep', 'row'), None, 'col'), parts along dimension 0, may hold values from -6 to 6
- lengths: int32 [8], P(('rep', 'row')), parts along dimension 0, may hold values from 256 to 2048, as said below
Outputs:
- attn_out: bfloat16 [8, 16384], P(('rep', 'col'), 'row'), parts along dimension 0
The draws below stay inside these ranges and needn't reach their ends.
There are 2 independent parts, one for each index of `rep`. The reference program is written for one: setup_inputs(seed, part) draws one part's arguments, and reference() takes and returns one part's arrays. A program takes and returns all parts, laid end to end along the dimension named above; an argument that names none is the same for every part. Nothing has to cross between parts.
Inputs may be any that keep to these rules, and one draw needn't show every extreme that they name: `lengths`: each length is at least 256 and at most 2048; some request has exactly 2048.
All inputs are finite; a program needn't handle non-finite values.
Results may differ from the reference program's by a relative error of at most 0.0055.
The reference program's roundings to bfloat16 on the way (of `normed`, `probs` and `heads_out`) count: a program that leaves them out, or rounds other values in their place, can miss the bound.
Values may be sent and summed in bfloat16 or wider, within the bound.
No kernel may reach another device: no remote copies, remote signals or barrier semaphores. Data moves between devices by JAX's collectives and lax.ppermute only.
A program may use at most 128 MiB of HBM per device.

```python
import jax
import jax.numpy as jnp
from jax import lax

MODEL_WIDTH = 16384
QUERY_HEADS = 64
KEY_VALUE_HEADS = 4
HEAD_WIDTH = 128
CACHE_SLOTS = 2048
REQUEST_COUNT = 4


def draw_lengths(key, part):
    key = jax.random.fold_in(key, 7)
    key_lens, key_pick = jax.random.split(key)
    drawn = jax.random.randint(key_lens, (REQUEST_COUNT,), max(CACHE_SLOTS // 8, 1), CACHE_SLOTS + 1)
    chosen = jax.random.randint(key_pick, (), 0, REQUEST_COUNT)
    drawn = jnp.where(jnp.arange(REQUEST_COUNT) == chosen, CACHE_SLOTS, drawn)
    return drawn.astype(jnp.int32)


def draw_stored_keys(key, part):
    key = jax.random.fold_in(key, 11)
    key_entries = jax.random.fold_in(key, 0)
    rotary_base = jnp.clip(jax.random.normal(key_entries, (REQUEST_COUNT, CACHE_SLOTS, KEY_VALUE_HEADS, HEAD_WIDTH), jnp.float32), -6.0, 6.0)
    return rotary_base.reshape(REQUEST_COUNT, CACHE_SLOTS, KEY_VALUE_HEADS * HEAD_WIDTH).astype(jnp.bfloat16)


def level_of(key, shape, pieces, low, top_value):
    gain, own = 1.0, jax.random.fold_in(key, 6)
    for dim, shards_of in pieces:
        heights = jnp.exp(jax.random.uniform(jax.random.fold_in(own, dim), (shards_of,), jnp.float32, low / len(pieces), top_value / len(pieces)))
        gain = gain * jnp.repeat(heights, shape[dim] // shards_of).reshape([-1 if axis == dim else 1 for axis in range(len(shape))])
    return gain


def gaussian(key, shape, deviation, most, cuts=(), kind=jnp.bfloat16):
    gain = level_of(key, shape, cuts, -0.22, 0.18) if cuts else 1.0
    values = jax.random.normal(key, shape, jnp.float32) * deviation * gain
    return jnp.minimum(jnp.maximum(values, -most), most).astype(kind)


def setup_inputs(seed: int = 0, part: int = 0) -> dict:
    seeds = jax.random.split(jax.random.key(seed), 10)
    part_splits = jax.random.split(jax.random.fold_in(seeds[9], part), 10)
    hidden_in = gaussian(part_splits[0], (REQUEST_COUNT, MODEL_WIDTH), 1.0, 6.0, ((1, 4),))
    norm_gain = jnp.clip(0.5 + 1.0 * jax.random.uniform(seeds[1], (MODEL_WIDTH,), jnp.float32) ** level_of(seeds[1], (MODEL_WIDTH,), ((0, 4),), -0.2, 0.2), 0.5, 1.5)
    w_query = gaussian(seeds[2], (MODEL_WIDTH, QUERY_HEADS * HEAD_WIDTH), MODEL_WIDTH ** -0.5, 0.046875, ((0, 4), (1, 4)))
    key_weight = gaussian(seeds[3], (MODEL_WIDTH, KEY_VALUE_HEADS * HEAD_WIDTH), MODEL_WIDTH ** -0.5, 0.046875, ((0, 4), (1, 4)))
    value_weight = gaussian(seeds[4], (MODEL_WIDTH, KEY_VALUE_HEADS * HEAD_WIDTH), MODEL_WIDTH ** -0.5, 0.046875, ((0, 4), (1, 4)))
    w_output = gaussian(seeds[5], (QUERY_HEADS * HEAD_WIDTH, MODEL_WIDTH), ((CACHE_SLOTS / (QUERY_HEADS * HEAD_WIDTH)) ** 0.5), 3.0, ((0, 4), (1, 4)))
    stored_keys = draw_stored_keys(jax.random.fold_in(jax.random.fold_in(seeds[9], part), 71), part)
    stored_values = gaussian(part_splits[7], (REQUEST_COUNT, CACHE_SLOTS, KEY_VALUE_HEADS * HEAD_WIDTH), 1.0, 6.0, ((0, 4), (2, 4)))
    lengths = draw_lengths(jax.random.fold_in(jax.random.fold_in(seeds[9], part), 71), part)
    return dict(hidden_in=hidden_in, norm_gain=norm_gain, w_query=w_query, key_weight=key_weight, value_weight=value_weight, w_output=w_output, stored_keys=stored_keys, stored_values=stored_values, lengths=lengths)


def apply_rotation(values, positions):
    half_dim = HEAD_WIDTH // 2
    frequency = 500000.0 ** (-(jnp.arange(half_dim, dtype=jnp.float32) * 2.0 / HEAD_WIDTH))
    angles = positions.astype(jnp.float32)[:, None] * frequency[None, :]
    cosine = jnp.cos(angles)[:, None, :]
    sine_part = jnp.sin(angles)[:, None, :]
    first = values[..., :half_dim]
    second = values[..., half_dim:]
    return jnp.concatenate([first * cosine - second * sine_part, second * cosine + first * sine_part], axis=-1)

def reference(hidden_in, norm_gain, w_query, key_weight, value_weight, w_output, stored_keys, stored_values, lengths):
    request_rows = hidden_in.shape[0]
    group_size = QUERY_HEADS // KEY_VALUE_HEADS
    inputs = hidden_in.astype(jnp.float32)
    row_scale = lax.rsqrt(lax.optimization_barrier(jnp.mean(inputs * inputs, axis=1)) + 1e-05)
    normed = (inputs * norm_gain[None, :]).astype(jnp.bfloat16)
    query = jnp.dot(normed, w_query, preferred_element_type=jnp.float32) * row_scale[:, None]
    fresh_key = jnp.dot(normed, key_weight, preferred_element_type=jnp.float32) * row_scale[:, None]
    fresh_value = jnp.dot(normed, value_weight, preferred_element_type=jnp.float32) * row_scale[:, None]
    query_rotated_rows = apply_rotation(query.reshape(request_rows, QUERY_HEADS, HEAD_WIDTH), lengths).astype(jnp.bfloat16)
    key_rotated_rows = apply_rotation(fresh_key.reshape(request_rows, KEY_VALUE_HEADS, HEAD_WIDTH), lengths).astype(jnp.bfloat16)
    value_request_rows = fresh_value.reshape(request_rows, KEY_VALUE_HEADS, HEAD_WIDTH).astype(jnp.bfloat16)
    query_groups = query_rotated_rows.reshape(request_rows, KEY_VALUE_HEADS, group_size, HEAD_WIDTH).astype(jnp.float32)
    every_key = stored_keys.reshape(request_rows, CACHE_SLOTS, KEY_VALUE_HEADS, HEAD_WIDTH).astype(jnp.float32)
    every_value = stored_values.reshape(request_rows, CACHE_SLOTS, KEY_VALUE_HEADS, HEAD_WIDTH).astype(jnp.float32)
    inverse = 1.0 / HEAD_WIDTH ** 0.5
    scores = jnp.einsum('rkgd,rckd->rkgc', query_groups, every_key) * inverse
    score_new = jnp.einsum('rkgd,rkd->rkg', query_groups, key_rotated_rows.astype(jnp.float32)) * inverse
    is_live = (jnp.arange(CACHE_SLOTS, dtype=jnp.int32)[None, :] < lengths[:, None])[:, None, None, :]
    largest = jnp.maximum(lax.optimization_barrier(jnp.max(jnp.where(is_live, scores, -jnp.inf), axis=-1)), score_new)
    expo = jnp.where(is_live, jnp.exp(scores - largest[..., None]), 0.0)
    expo_new = jnp.exp(score_new - largest)
    denom = lax.optimization_barrier(jnp.sum(expo, axis=-1)) + expo_new
    probs = (expo / denom[..., None]).astype(jnp.bfloat16)
    prob_new = (expo_new / denom).astype(jnp.bfloat16)
    heads_out = jnp.einsum('rkgc,rckd->rkgd', probs.astype(jnp.float32), every_value)
    heads_out = heads_out + prob_new.astype(jnp.float32)[..., None] * value_request_rows.astype(jnp.float32)[:, :, None, :]
    heads_out = heads_out.astype(jnp.bfloat16).reshape(request_rows, QUERY_HEADS * HEAD_WIDTH)
    return jnp.dot(heads_out, w_output, preferred_element_type=jnp.float32).astype(jnp.bfloat16)
```

```python
import functools

import jax
import jax.numpy as jnp
from jax import lax
from jax.sharding import PartitionSpec as P

MODEL_WIDTH = 16384
QUERY_HEADS = 64
KEY_VALUE_HEADS = 4
HEAD_WIDTH = 128


def apply_rotation(values, positions):
    half_dim = values.shape[-1] // 2
    head_size = values.shape[-1]
    frequency = 500000.0 ** (-(jnp.arange(half_dim, dtype=jnp.float32) * 2.0 / head_size))
    angles = positions.astype(jnp.float32)[:, None] * frequency[None, :]
    cosine = jnp.cos(angles)[:, None, :]
    sine_part = jnp.sin(angles)[:, None, :]
    first = values[..., :half_dim]
    second = values[..., half_dim:]
    return jnp.concatenate(
        [first * cosine - second * sine_part, second * cosine + first * sine_part], axis=-1
    )


DIRECT_LIMIT = 8


def is_direct(size):
    return 1 < size <= DIRECT_LIMIT and size & (size - 1) == 0


def partner_order(size):
    return range(size - 1, 0, -1)


def swap_with(values, axis, size, mask):
    return lax.ppermute(values, axis, [(i, i ^ mask) for i in range(size)])


def scatter_sum(values, axis, size):
    if not is_direct(size):
        return lax.psum_scatter(values, axis, scatter_dimension=0, tiled=True)
    share = values.shape[0] // size
    me = lax.axis_index(axis)
    total = lax.dynamic_slice_in_dim(values, me * share, share, 0)
    received = [
        swap_with(
            lax.dynamic_slice_in_dim(values, (me ^ mask) * share, share, 0), axis, size, mask
        )
        for mask in partner_order(size)
    ]
    for part in received:
        total = total + part
    return total


def gather_rows(values, axis, size):
    if not is_direct(size):
        return lax.all_gather(values, axis, axis=0, tiled=True)
    me = lax.axis_index(axis)
    blocks = [values] * size
    for mask in partner_order(size):
        blocks[mask] = swap_with(values, axis, size, mask)
    ordered = []
    for place in range(size):
        block = blocks[0]
        for mask in range(1, size):
            block = jnp.where((me ^ mask) == place, blocks[mask], block)
        ordered.append(block)
    return jnp.concatenate(ordered, axis=0)


def body(
    row_size,
    col_size,
    hidden_in,
    norm_gain,
    w_query,
    key_weight,
    value_weight,
    w_output,
    stored_keys,
    stored_values,
    lengths,
):
    per_device = stored_keys.shape[0]
    capacity = stored_keys.shape[1]
    group_size = QUERY_HEADS // KEY_VALUE_HEADS
    head_size = HEAD_WIDTH
    kv_heads = stored_keys.shape[2] // head_size
    query_width = w_query.shape[1]
    kv_width = key_weight.shape[1]
    inputs = hidden_in.astype(jnp.float32)
    squares = jnp.sum(inputs * inputs, axis=1, keepdims=True)
    normed = (inputs * norm_gain[None, :]).astype(jnp.bfloat16)
    weights_all = jnp.concatenate([w_query, key_weight, value_weight], axis=1)
    partial_all = jnp.dot(normed, weights_all, preferred_element_type=jnp.float32)
    lanes = jnp.broadcast_to(squares, (squares.shape[0], head_size))
    projected = scatter_sum(jnp.concatenate([partial_all, lanes], axis=1), "row", row_size)
    my_scale = lax.rsqrt(projected[:, query_width + 2 * kv_width :][:, :1] / MODEL_WIDTH + 1e-05)
    query_part = projected[:, :query_width]
    key_part = projected[:, query_width : query_width + kv_width]
    value_part = projected[:, query_width + kv_width : query_width + 2 * kv_width]
    query_rotated_rows = apply_rotation(
        (query_part * my_scale).reshape(per_device, kv_heads * group_size, head_size), lengths
    )
    query_rotated_rows = query_rotated_rows.astype(jnp.bfloat16).reshape(
        per_device, kv_heads, group_size, head_size
    )
    key_rotated_rows = apply_rotation(
        (key_part * my_scale).reshape(per_device, kv_heads, head_size), lengths
    ).astype(jnp.bfloat16)
    value_request_rows = (
        (value_part * my_scale).reshape(per_device, kv_heads, head_size).astype(jnp.bfloat16)
    )
    every_key = stored_keys.reshape(per_device, capacity, kv_heads, head_size)
    every_value = stored_values.reshape(per_device, capacity, kv_heads, head_size)
    inverse = 1.0 / head_size**0.5
    score_new = (
        jnp.einsum(
            "rkgd,rkd->rkg",
            query_rotated_rows,
            key_rotated_rows,
            preferred_element_type=jnp.float32,
        )
        * inverse
    )
    tail_new = value_request_rows.astype(jnp.float32)[:, :, None, :]
    scores = (
        jnp.einsum(
            "rkgd,rckd->rkgc", query_rotated_rows, every_key, preferred_element_type=jnp.float32
        )
        * inverse
    )
    is_live = (jnp.arange(capacity, dtype=jnp.int32)[None, :] < lengths[:, None])[:, None, None, :]
    largest = jnp.maximum(jnp.max(jnp.where(is_live, scores, -jnp.inf), axis=-1), score_new)
    expo = jnp.where(is_live, jnp.exp(scores - largest[..., None]), 0.0)
    expo_new = jnp.exp(score_new - largest)
    denom = jnp.sum(expo, axis=-1) + expo_new
    probs = (expo / denom[..., None]).astype(jnp.bfloat16)
    prob_new = (expo_new / denom).astype(jnp.bfloat16)
    heads_out = jnp.einsum(
        "rkgc,rckd->rkgd", probs, every_value, preferred_element_type=jnp.float32
    )
    heads_out = heads_out + prob_new.astype(jnp.float32)[..., None] * tail_new
    heads_out = heads_out.astype(jnp.bfloat16).reshape(
        per_device, kv_heads * group_size * head_size
    )
    partial_out = jnp.dot(
        gather_rows(heads_out, "row", row_size),
        w_output,
        preferred_element_type=jnp.float32,
    )
    return scatter_sum(partial_out, "col", col_size).astype(jnp.bfloat16)


def solution(mesh):
    placed = (
        P("rep", "row"),
        P("row"),
        P("row", "col"),
        P("row", "col"),
        P("row", "col"),
        P("col", "row"),
        P(("rep", "row"), None, "col"),
        P(("rep", "row"), None, "col"),
        P(("rep", "row")),
    )
    sized = functools.partial(body, mesh.shape["row"], mesh.shape["col"])
    return jax.shard_map(
        sized, mesh=mesh, in_specs=placed, out_specs=P(("rep", "col"), "row"), check_vma=False
    )
```

```python
import functools

import jax
import jax.numpy as jnp
from jax import lax
from jax.experimental import pallas as pl
from jax.experimental.pallas import tpu as pltpu
from jax.sharding import PartitionSpec as P

MODEL_WIDTH = 16384
QUERY_HEADS = 64
KEY_VALUE_HEADS = 4
HEAD_WIDTH = 128
REQUEST_COUNT = 4


def apply_rotation(values, positions):
    half_dim = values.shape[-1] // 2
    head_size = values.shape[-1]
    frequency = 500000.0 ** (-(jnp.arange(half_dim, dtype=jnp.float32) * 2.0 / head_size))
    angles = positions.astype(jnp.float32)[:, None] * frequency[None, :]
    cosine = jnp.cos(angles)[:, None, :]
    sine_part = jnp.sin(angles)[:, None, :]
    first = values[..., :half_dim]
    second = values[..., half_dim:]
    return jnp.concatenate(
        [first * cosine - second * sine_part, second * cosine + first * sine_part], axis=-1
    )


DIRECT_LIMIT = 8
MIB = 1024 * 1024
VMEM_HELD = 26 * MIB
PRIORITY = 1
BLOCK = 512
AHEAD = 4


def is_direct(size):
    return 1 < size <= DIRECT_LIMIT and size & (size - 1) == 0


def partner_order(size):
    return range(size - 1, 0, -1)


def swap_with(values, axis, size, mask):
    return lax.ppermute(values, axis, [(i, i ^ mask) for i in range(size)])


def scatter_sum(values, axis, size):
    if not is_direct(size):
        return lax.psum_scatter(values, axis, scatter_dimension=0, tiled=True)
    share = values.shape[0] // size
    me = lax.axis_index(axis)
    total = lax.dynamic_slice_in_dim(values, me * share, share, 0)
    received = [
        swap_with(
            lax.dynamic_slice_in_dim(values, (me ^ mask) * share, share, 0), axis, size, mask
        )
        for mask in partner_order(size)
    ]
    for part in received:
        total = total + part
    return total


def gather_rows(values, axis, size):
    if not is_direct(size):
        return lax.all_gather(values, axis, axis=0, tiled=True)
    me = lax.axis_index(axis)
    blocks = [values] * size
    for mask in partner_order(size):
        blocks[mask] = swap_with(values, axis, size, mask)
    ordered = []
    for place in range(size):
        block = blocks[0]
        for mask in range(1, size):
            block = jnp.where((me ^ mask) == place, blocks[mask], block)
        ordered.append(block)
    return jnp.concatenate(ordered, axis=0)


def in_hbm(array):
    return pltpu.with_memory_space_constraint(array, pltpu.HBM)


def project_kernel(row_size, block, ahead, hidden, gain, w_query, w_key, w_value, *refs):
    shares = refs[:row_size]
    inputs_near, gain_near, query_buffer, key_buffer, value_buffer, sems, small, left, total = refs[
        row_size:
    ]
    requests, depth = hidden.shape
    query_width, kv_width = w_query.shape[1], w_key.shape[1]
    steps = depth // block
    wide = depth // min(4, steps)
    first = [
        pltpu.make_async_copy(hidden, inputs_near, small.at[0]),
        pltpu.make_async_copy(gain, gain_near, small.at[1]),
    ]
    stages = []
    for step in range(steps):
        start = step * block
        group = []
        if start % wide == 0:
            rows = pl.ds(start, wide)
            for lane, (far, near) in enumerate(((w_key, key_buffer), (w_value, value_buffer))):
                copy = pltpu.make_async_copy(
                    far.at[rows], near.at[rows], sems.at[1 + lane, start // wide]
                )
                group.append((copy, 1 + lane, near, start, wide))
        rows = pl.ds(start, block)
        copy = pltpu.make_async_copy(w_query.at[rows], query_buffer.at[rows], sems.at[0, step])
        group.append((copy, 0, query_buffer, start, block))
        stages.append(group)
    for copy in first:
        copy.start()
    for group in stages[:ahead]:
        for item in group:
            item[0].start(priority=PRIORITY)
    for copy in first:
        copy.wait()
    inputs = inputs_near[...].astype(jnp.float32)
    left[...] = jnp.zeros_like(left)
    left[:requests, :] = inputs * gain_near[...]
    normed = left[...].astype(jnp.bfloat16)
    squares = jnp.sum(inputs * inputs, axis=1, keepdims=True)
    sums = [None, None, None]
    for step, group in enumerate(stages):
        for copy, which, near, start, size in group:
            copy.wait()
            if which == 0 and step + ahead < steps:
                for item in stages[step + ahead]:
                    item[0].start(priority=PRIORITY)
            part = jnp.dot(
                normed[:, start : start + size],
                near[start : start + size, :],
                preferred_element_type=jnp.float32,
            )
            sums[which] = part if sums[which] is None else sums[which] + part
    total[:, :query_width] = sums[0]
    total[:, query_width : query_width + kv_width] = sums[1]
    total[:, query_width + kv_width : query_width + 2 * kv_width] = sums[2]
    total[:requests, query_width + 2 * kv_width :] = jnp.broadcast_to(
        squares, (requests, HEAD_WIDTH)
    )
    here = lax.axis_index("row")
    for mask in range(row_size):
        shares[mask][...] = total[pl.ds(here ^ mask, 1), :]


def project_in(hidden_in, norm_gain, w_query, key_weight, value_weight):
    row_size = hidden_in.shape[0]
    depth, query_width = w_query.shape
    kv_width = key_weight.shape[1]
    block = min(depth, BLOCK)
    steps = depth // block
    width = query_width + 2 * kv_width + HEAD_WIDTH
    near = pl.BlockSpec(memory_space=pltpu.VMEM)
    far = pl.BlockSpec(memory_space=pltpu.HBM)
    size = 2 * depth * (query_width + 2 * kv_width)
    return pl.pallas_call(
        functools.partial(project_kernel, row_size, block, AHEAD),
        out_shape=[jax.ShapeDtypeStruct((1, width), jnp.float32)] * row_size,
        in_specs=[far] * 5,
        out_specs=[near] * row_size,
        scratch_shapes=[
            pltpu.VMEM((row_size, depth), jnp.bfloat16),
            pltpu.VMEM((1, depth), jnp.float32),
            pltpu.VMEM((depth, query_width), jnp.bfloat16),
            pltpu.VMEM((depth, kv_width), jnp.bfloat16),
            pltpu.VMEM((depth, kv_width), jnp.bfloat16),
            pltpu.SemaphoreType.DMA((3, steps)),
            pltpu.SemaphoreType.DMA((2,)),
            pltpu.VMEM((8, depth), jnp.float32),
            pltpu.VMEM((8, width), jnp.float32),
        ],
        compiler_params=pltpu.CompilerParams(vmem_limit_bytes=VMEM_HELD),
        cost_estimate=pl.CostEstimate(
            flops=row_size * size, bytes_accessed=size, transcendentals=0
        ),
        name="project_in",
    )(*map(in_hbm, (hidden_in, norm_gain.reshape(1, depth), w_query, key_weight, value_weight)))


def attend_kernel(row_size, *refs):
    shares = refs[:row_size]
    length, cosine, sine, keys, values, heads, rows = refs[row_size:]
    heads_count, width = heads.shape
    summed = shares[0][...]
    for part in shares[1:]:
        summed = summed + part[...]
    query_width = heads_count * width
    squares = summed[:, query_width + 2 * width :]
    scale = lax.rsqrt(squares / MODEL_WIDTH + 1e-05)
    for head in range(heads_count):
        rows[head : head + 1, :] = summed[:, head * width : (head + 1) * width] * scale
    key_row = summed[:, query_width : query_width + width] * scale
    value_row = summed[:, query_width + width : query_width + 2 * width] * scale
    rows[heads_count : heads_count + 8, :] = jnp.broadcast_to(key_row, (8, width))
    both = rows[...]
    turned = both * cosine[...] + pltpu.roll(both, width // 2, 1) * sine[...]
    turned = turned.astype(jnp.bfloat16)
    query = turned[:heads_count]
    key_new = turned[heads_count : heads_count + 8].astype(jnp.float32)[:1]
    value_new = value_row.astype(jnp.bfloat16).astype(jnp.float32)
    inverse = 1.0 / width**0.5
    scores = (
        lax.dot_general(
            query, keys[...], (((1,), (1,)), ((), ())), preferred_element_type=jnp.float32
        )
        * inverse
    )
    score_new = (
        jnp.sum(query.astype(jnp.float32) * key_new, axis=1, keepdims=True) * inverse
    )
    place = lax.broadcasted_iota(jnp.int32, scores.shape, 1)
    live = place < length[0]
    scores = jnp.where(live, scores, -jnp.inf)
    largest = jnp.maximum(jnp.max(scores, axis=1, keepdims=True), score_new)
    expo = jnp.exp(scores - largest)
    expo_new = jnp.exp(score_new - largest)
    part = 1.0 / (jnp.sum(expo, axis=1, keepdims=True) + expo_new)
    probs = (expo * part).astype(jnp.bfloat16)
    prob_new = (expo_new * part).astype(jnp.bfloat16).astype(jnp.float32)
    mixed = jnp.dot(probs, values[...], preferred_element_type=jnp.float32)
    heads[...] = (mixed + prob_new * value_new).astype(jnp.bfloat16)


def attend(shares, lengths, keys, values, heads_count):
    row_size = len(shares)
    slots, width = keys.shape
    half = width // 2
    frequency = 500000.0 ** (-(jnp.arange(half, dtype=jnp.float32) * 2.0 / width))
    angles = lengths.astype(jnp.float32)[:, None] * frequency[None, :]
    cosine, sine = jnp.cos(angles), jnp.sin(angles)
    cosine = jnp.concatenate([cosine, cosine], axis=1)
    sine = jnp.concatenate([-sine, sine], axis=1)
    near = pl.BlockSpec(memory_space=pltpu.VMEM)
    return pl.pallas_call(
        functools.partial(attend_kernel, row_size),
        out_shape=jax.ShapeDtypeStruct((heads_count, width), jnp.bfloat16),
        in_specs=[near] * row_size + [pl.BlockSpec(memory_space=pltpu.SMEM)] + [near] * 4,
        out_specs=near,
        scratch_shapes=[pltpu.VMEM((heads_count + 8, width), jnp.float32)],
        compiler_params=pltpu.CompilerParams(vmem_limit_bytes=4 * MIB),
        cost_estimate=pl.CostEstimate(
            flops=4 * heads_count * slots * width,
            bytes_accessed=4 * slots * width,
            transcendentals=heads_count * slots,
        ),
        name="attend",
    )(*shares, lengths, cosine, sine, keys, values)


def output_kernel(row_size, col_size, chunk, *refs):
    heads = refs[:row_size]
    weight = refs[row_size]
    shares = refs[row_size + 1 : row_size + 1 + col_size]
    left, total = refs[row_size + 1 + col_size :]
    count = heads[0].shape[0]
    width = heads[0].shape[1]
    left[...] = jnp.zeros_like(left)
    for slot in range(row_size):
        rows = heads[slot][...].astype(jnp.float32)
        for head in range(count):
            left[slot : slot + 1, head * width : (head + 1) * width] = rows[head : head + 1, :]
    lhs = left[...].astype(jnp.bfloat16)
    for start in range(0, weight.shape[1], chunk):
        total[:, start : start + chunk] = jnp.dot(
            lhs, weight[:, start : start + chunk], preferred_element_type=jnp.float32
        )
    here = lax.axis_index("row")
    lane = lax.axis_index("col")
    for mask in range(col_size):
        shares[mask][...] = total[pl.ds((lane ^ mask) ^ here, 1), :]


def project_out(blocks, w_output, col_size):
    row_size = len(blocks)
    depth, width = w_output.shape
    whole = pl.BlockSpec(memory_space=pltpu.VMEM)
    return pl.pallas_call(
        functools.partial(output_kernel, row_size, col_size, min(width, 512)),
        out_shape=[jax.ShapeDtypeStruct((1, width), jnp.float32)] * col_size,
        in_specs=[whole] * (row_size + 1),
        out_specs=[whole] * col_size,
        scratch_shapes=[
            pltpu.VMEM((8, depth), jnp.float32),
            pltpu.VMEM((8, width), jnp.float32),
        ],
        compiler_params=pltpu.CompilerParams(vmem_limit_bytes=4 * MIB),
        cost_estimate=pl.CostEstimate(
            flops=2 * row_size * depth * width, bytes_accessed=2 * depth * width, transcendentals=0
        ),
        name="project_out",
    )(*blocks, w_output)


def body(
    row_size,
    col_size,
    hidden_in,
    norm_gain,
    w_query,
    key_weight,
    value_weight,
    w_output,
    stored_keys,
    stored_values,
    lengths,
):
    per_device = stored_keys.shape[0]
    capacity = stored_keys.shape[1]
    group_size = QUERY_HEADS // KEY_VALUE_HEADS
    head_size = HEAD_WIDTH
    kv_heads = stored_keys.shape[2] // head_size
    query_width = w_query.shape[1]
    kv_width = key_weight.shape[1]
    inputs = hidden_in.astype(jnp.float32)
    squares = jnp.sum(inputs * inputs, axis=1, keepdims=True)
    normed = (inputs * norm_gain[None, :]).astype(jnp.bfloat16)
    weights_all = jnp.concatenate([w_query, key_weight, value_weight], axis=1)
    partial_all = jnp.dot(normed, weights_all, preferred_element_type=jnp.float32)
    lanes = jnp.broadcast_to(squares, (squares.shape[0], head_size))
    projected = scatter_sum(jnp.concatenate([partial_all, lanes], axis=1), "row", row_size)
    my_scale = lax.rsqrt(projected[:, query_width + 2 * kv_width :][:, :1] / MODEL_WIDTH + 1e-05)
    query_part = projected[:, :query_width]
    key_part = projected[:, query_width : query_width + kv_width]
    value_part = projected[:, query_width + kv_width : query_width + 2 * kv_width]
    query_rotated_rows = apply_rotation(
        (query_part * my_scale).reshape(per_device, kv_heads * group_size, head_size), lengths
    )
    query_rotated_rows = query_rotated_rows.astype(jnp.bfloat16).reshape(
        per_device, kv_heads, group_size, head_size
    )
    key_rotated_rows = apply_rotation(
        (key_part * my_scale).reshape(per_device, kv_heads, head_size), lengths
    ).astype(jnp.bfloat16)
    value_request_rows = (
        (value_part * my_scale).reshape(per_device, kv_heads, head_size).astype(jnp.bfloat16)
    )
    every_key = stored_keys.reshape(per_device, capacity, kv_heads, head_size)
    every_value = stored_values.reshape(per_device, capacity, kv_heads, head_size)
    inverse = 1.0 / head_size**0.5
    score_new = (
        jnp.einsum(
            "rkgd,rkd->rkg",
            query_rotated_rows,
            key_rotated_rows,
            preferred_element_type=jnp.float32,
        )
        * inverse
    )
    tail_new = value_request_rows.astype(jnp.float32)[:, :, None, :]
    scores = (
        jnp.einsum(
            "rkgd,rckd->rkgc", query_rotated_rows, every_key, preferred_element_type=jnp.float32
        )
        * inverse
    )
    is_live = (jnp.arange(capacity, dtype=jnp.int32)[None, :] < lengths[:, None])[:, None, None, :]
    largest = jnp.maximum(jnp.max(jnp.where(is_live, scores, -jnp.inf), axis=-1), score_new)
    expo = jnp.where(is_live, jnp.exp(scores - largest[..., None]), 0.0)
    expo_new = jnp.exp(score_new - largest)
    denom = jnp.sum(expo, axis=-1) + expo_new
    probs = (expo / denom[..., None]).astype(jnp.bfloat16)
    prob_new = (expo_new / denom).astype(jnp.bfloat16)
    heads_out = jnp.einsum(
        "rkgc,rckd->rkgd", probs, every_value, preferred_element_type=jnp.float32
    )
    heads_out = heads_out + prob_new.astype(jnp.float32)[..., None] * tail_new
    heads_out = heads_out.astype(jnp.bfloat16).reshape(
        per_device, kv_heads * group_size * head_size
    )
    partial_out = jnp.dot(
        gather_rows(heads_out, "row", row_size),
        w_output,
        preferred_element_type=jnp.float32,
    )
    return scatter_sum(partial_out, "col", col_size).astype(jnp.bfloat16)


def direct_body(
    size,
    hidden_in,
    norm_gain,
    w_query,
    key_weight,
    value_weight,
    w_output,
    stored_keys,
    stored_values,
    lengths,
):
    head_size = HEAD_WIDTH
    parts = project_in(hidden_in, norm_gain, w_query, key_weight, value_weight)
    shares = [parts[0]] + [
        swap_with(parts[mask], "row", size, mask) for mask in partner_order(size)
    ]
    mine = attend(
        shares, lengths, stored_keys[0], stored_values[0], w_query.shape[1] // head_size
    )
    blocks = [mine] + [None] * (size - 1)
    for mask in partner_order(size):
        blocks[mask] = swap_with(mine, "row", size, mask)
    parts = project_out(blocks, w_output, size)
    received = [swap_with(parts[mask], "col", size, mask) for mask in partner_order(size)]
    total = parts[0]
    for part in received:
        total = total + part
    return total.astype(jnp.bfloat16)


def fits_direct(mesh):
    size = mesh.shape["row"]
    return is_direct(size) and size == mesh.shape["col"] == KEY_VALUE_HEADS == REQUEST_COUNT


def solution(mesh):
    placed = (
        P("rep", "row"),
        P("row"),
        P("row", "col"),
        P("row", "col"),
        P("row", "col"),
        P("col", "row"),
        P(("rep", "row"), None, "col"),
        P(("rep", "row"), None, "col"),
        P(("rep", "row")),
    )
    if fits_direct(mesh):
        sized = functools.partial(direct_body, mesh.shape["row"])
    else:
        sized = functools.partial(body, mesh.shape["row"], mesh.shape["col"])
    return jax.shard_map(
        sized, mesh=mesh, in_specs=placed, out_specs=P(("rep", "col"), "row"), check_vma=False
    )
```

```python
import functools

import jax
import jax.numpy as jnp
from jax import lax
from jax.experimental import pallas as pl
from jax.experimental.pallas import tpu as pltpu
from jax.sharding import PartitionSpec as P

MODEL_WIDTH = 16384
QUERY_HEADS = 64
KEY_VALUE_HEADS = 4
HEAD_WIDTH = 128
REQUEST_COUNT = 4


def apply_rotation(values, positions):
    half_dim = values.shape[-1] // 2
    head_size = values.shape[-1]
    frequency = 500000.0 ** (-(jnp.arange(half_dim, dtype=jnp.float32) * 2.0 / head_size))
    angles = positions.astype(jnp.float32)[:, None] * frequency[None, :]
    cosine = jnp.cos(angles)[:, None, :]
    sine_part = jnp.sin(angles)[:, None, :]
    first = values[..., :half_dim]
    second = values[..., half_dim:]
    return jnp.concatenate(
        [first * cosine - second * sine_part, second * cosine + first * sine_part], axis=-1
    )


DIRECT_LIMIT = 8
MIB = 1024 * 1024
VMEM_HELD = 26 * MIB
PRIORITY = 1
BLOCK = 1024
TAIL = 128


def is_direct(size):
    return 1 < size <= DIRECT_LIMIT and size & (size - 1) == 0


def partner_order(size):
    return range(size - 1, 0, -1)


def swap_with(values, axis, size, mask):
    return lax.ppermute(values, axis, [(i, i ^ mask) for i in range(size)])


def scatter_sum(values, axis, size):
    if not is_direct(size):
        return lax.psum_scatter(values, axis, scatter_dimension=0, tiled=True)
    share = values.shape[0] // size
    me = lax.axis_index(axis)
    total = lax.dynamic_slice_in_dim(values, me * share, share, 0)
    received = [
        swap_with(
            lax.dynamic_slice_in_dim(values, (me ^ mask) * share, share, 0), axis, size, mask
        )
        for mask in partner_order(size)
    ]
    for part in received:
        total = total + part
    return total


def gather_rows(values, axis, size):
    if not is_direct(size):
        return lax.all_gather(values, axis, axis=0, tiled=True)
    me = lax.axis_index(axis)
    blocks = [values] * size
    for mask in partner_order(size):
        blocks[mask] = swap_with(values, axis, size, mask)
    ordered = []
    for place in range(size):
        block = blocks[0]
        for mask in range(1, size):
            block = jnp.where((me ^ mask) == place, blocks[mask], block)
        ordered.append(block)
    return jnp.concatenate(ordered, axis=0)


def in_hbm(array):
    return pltpu.with_memory_space_constraint(array, pltpu.HBM)


def block_starts(depth):
    blocks = []
    start = 0
    while start < depth:
        size = min(BLOCK, depth - start)
        while size > TAIL and size * 2 > depth - start:
            size //= 2
        blocks.append((start, size))
        start += size
    return blocks


def project_kernel(row_size, blocks, hidden, gain, w_query, w_key, w_value, *refs):
    shares = refs[:row_size]
    inputs_near, gain_near, query_buffer, key_buffer, value_buffer, sems, left, total = refs[
        row_size:
    ]
    requests, depth = hidden.shape
    query_width, kv_width = w_query.shape[1], w_key.shape[1]
    first = [
        pltpu.make_async_copy(hidden, inputs_near, sems.at[0]),
        pltpu.make_async_copy(gain, gain_near, sems.at[1]),
    ]
    stages = [
        (pltpu.make_async_copy(w_key, key_buffer, sems.at[2]), 1, key_buffer, 0, depth),
        (pltpu.make_async_copy(w_value, value_buffer, sems.at[3]), 2, value_buffer, 0, depth),
    ]
    for step, (start, size) in enumerate(blocks):
        rows = pl.ds(start, size)
        copy = pltpu.make_async_copy(
            w_query.at[rows], query_buffer.at[rows], sems.at[4 + step]
        )
        stages.append((copy, 0, query_buffer, start, size))
    for copy in first:
        copy.start()
    for stage in stages:
        stage[0].start(priority=PRIORITY)
    for copy in first:
        copy.wait()
    inputs = inputs_near[...].astype(jnp.float32)
    left[...] = jnp.zeros_like(left)
    left[:requests, :] = inputs * gain_near[...]
    normed = left[...].astype(jnp.bfloat16)
    squares = jnp.sum(inputs * inputs, axis=1, keepdims=True)
    total[:requests, query_width + 2 * kv_width :] = jnp.broadcast_to(
        squares, (requests, HEAD_WIDTH)
    )
    sums = [None, None, None]
    for copy, which, near, start, size in stages:
        copy.wait()
        part = jnp.dot(
            normed[:, start : start + size],
            near[start : start + size, :],
            preferred_element_type=jnp.float32,
        )
        sums[which] = part if sums[which] is None else sums[which] + part
    total[:, query_width : query_width + kv_width] = sums[1]
    total[:, query_width + kv_width : query_width + 2 * kv_width] = sums[2]
    total[:, :query_width] = sums[0]
    here = lax.axis_index("row")
    for mask in range(row_size):
        shares[mask][...] = total[pl.ds(here ^ mask, 1), :]


def project_in(hidden_in, norm_gain, w_query, key_weight, value_weight):
    row_size = hidden_in.shape[0]
    depth, query_width = w_query.shape
    kv_width = key_weight.shape[1]
    blocks = block_starts(depth)
    width = query_width + 2 * kv_width + HEAD_WIDTH
    near = pl.BlockSpec(memory_space=pltpu.VMEM)
    far = pl.BlockSpec(memory_space=pltpu.HBM)
    size = 2 * depth * (query_width + 2 * kv_width)
    return pl.pallas_call(
        functools.partial(project_kernel, row_size, blocks),
        out_shape=[jax.ShapeDtypeStruct((1, width), jnp.float32)] * row_size,
        in_specs=[far] * 5,
        out_specs=[near] * row_size,
        scratch_shapes=[
            pltpu.VMEM((row_size, depth), jnp.bfloat16),
            pltpu.VMEM((1, depth), jnp.float32),
            pltpu.VMEM((depth, query_width), jnp.bfloat16),
            pltpu.VMEM((depth, kv_width), jnp.bfloat16),
            pltpu.VMEM((depth, kv_width), jnp.bfloat16),
            pltpu.SemaphoreType.DMA((4 + len(blocks),)),
            pltpu.VMEM((8, depth), jnp.float32),
            pltpu.VMEM((8, width), jnp.float32),
        ],
        compiler_params=pltpu.CompilerParams(vmem_limit_bytes=VMEM_HELD),
        cost_estimate=pl.CostEstimate(
            flops=row_size * size, bytes_accessed=size, transcendentals=0
        ),
        name="project_in",
    )(*map(in_hbm, (hidden_in, norm_gain.reshape(1, depth), w_query, key_weight, value_weight)))


def attend_kernel(row_size, *refs):
    shares = refs[:row_size]
    length, cosine, sine, keys, values, heads, rows = refs[row_size:]
    heads_count, width = heads.shape
    summed = shares[0][...]
    for part in shares[1:]:
        summed = summed + part[...]
    query_width = heads_count * width
    squares = summed[:, query_width + 2 * width :]
    scale = lax.rsqrt(squares / MODEL_WIDTH + 1e-05)
    for head in range(heads_count):
        rows[head : head + 1, :] = summed[:, head * width : (head + 1) * width] * scale
    key_row = summed[:, query_width : query_width + width] * scale
    value_row = summed[:, query_width + width : query_width + 2 * width] * scale
    rows[heads_count : heads_count + 8, :] = jnp.broadcast_to(key_row, (8, width))
    both = rows[...]
    turned = both * cosine[...] + pltpu.roll(both, width // 2, 1) * sine[...]
    turned = turned.astype(jnp.bfloat16)
    query = turned[:heads_count]
    key_new = turned[heads_count : heads_count + 8].astype(jnp.float32)[:1]
    value_new = value_row.astype(jnp.bfloat16).astype(jnp.float32)
    inverse = 1.0 / width**0.5
    scores = (
        lax.dot_general(
            query, keys[...], (((1,), (1,)), ((), ())), preferred_element_type=jnp.float32
        )
        * inverse
    )
    score_new = (
        jnp.sum(query.astype(jnp.float32) * key_new, axis=1, keepdims=True) * inverse
    )
    place = lax.broadcasted_iota(jnp.int32, scores.shape, 1)
    live = place < length[0]
    scores = jnp.where(live, scores, -jnp.inf)
    largest = jnp.maximum(jnp.max(scores, axis=1, keepdims=True), score_new)
    expo = jnp.exp(scores - largest)
    expo_new = jnp.exp(score_new - largest)
    part = 1.0 / (jnp.sum(expo, axis=1, keepdims=True) + expo_new)
    probs = (expo * part).astype(jnp.bfloat16)
    prob_new = (expo_new * part).astype(jnp.bfloat16).astype(jnp.float32)
    mixed = jnp.dot(probs, values[...], preferred_element_type=jnp.float32)
    heads[...] = (mixed + prob_new * value_new).astype(jnp.bfloat16)


def attend(shares, lengths, keys, values, heads_count):
    row_size = len(shares)
    slots, width = keys.shape
    half = width // 2
    frequency = 500000.0 ** (-(jnp.arange(half, dtype=jnp.float32) * 2.0 / width))
    angles = lengths.astype(jnp.float32)[:, None] * frequency[None, :]
    cosine, sine = jnp.cos(angles), jnp.sin(angles)
    cosine = jnp.concatenate([cosine, cosine], axis=1)
    sine = jnp.concatenate([-sine, sine], axis=1)
    near = pl.BlockSpec(memory_space=pltpu.VMEM)
    return pl.pallas_call(
        functools.partial(attend_kernel, row_size),
        out_shape=jax.ShapeDtypeStruct((heads_count, width), jnp.bfloat16),
        in_specs=[near] * row_size + [pl.BlockSpec(memory_space=pltpu.SMEM)] + [near] * 4,
        out_specs=near,
        scratch_shapes=[pltpu.VMEM((heads_count + 8, width), jnp.float32)],
        compiler_params=pltpu.CompilerParams(vmem_limit_bytes=4 * MIB),
        cost_estimate=pl.CostEstimate(
            flops=4 * heads_count * slots * width,
            bytes_accessed=4 * slots * width,
            transcendentals=heads_count * slots,
        ),
        name="attend",
    )(*shares, lengths, cosine, sine, keys, values)


def output_kernel(row_size, col_size, chunk, *refs):
    heads = refs[:row_size]
    weight = refs[row_size]
    shares = refs[row_size + 1 : row_size + 1 + col_size]
    left, total = refs[row_size + 1 + col_size :]
    count = heads[0].shape[0]
    width = heads[0].shape[1]
    left[...] = jnp.zeros_like(left)
    for slot in range(row_size):
        rows = heads[slot][...].astype(jnp.float32)
        for head in range(count):
            left[slot : slot + 1, head * width : (head + 1) * width] = rows[head : head + 1, :]
    lhs = left[...].astype(jnp.bfloat16)
    for start in range(0, weight.shape[1], chunk):
        total[:, start : start + chunk] = jnp.dot(
            lhs, weight[:, start : start + chunk], preferred_element_type=jnp.float32
        )
    here = lax.axis_index("row")
    lane = lax.axis_index("col")
    for mask in range(col_size):
        shares[mask][...] = total[pl.ds((lane ^ mask) ^ here, 1), :]


def project_out(blocks, w_output, col_size):
    row_size = len(blocks)
    depth, width = w_output.shape
    whole = pl.BlockSpec(memory_space=pltpu.VMEM)
    return pl.pallas_call(
        functools.partial(output_kernel, row_size, col_size, min(width, 512)),
        out_shape=[jax.ShapeDtypeStruct((1, width), jnp.float32)] * col_size,
        in_specs=[whole] * (row_size + 1),
        out_specs=[whole] * col_size,
        scratch_shapes=[
            pltpu.VMEM((8, depth), jnp.float32),
            pltpu.VMEM((8, width), jnp.float32),
        ],
        compiler_params=pltpu.CompilerParams(vmem_limit_bytes=4 * MIB),
        cost_estimate=pl.CostEstimate(
            flops=2 * row_size * depth * width, bytes_accessed=2 * depth * width, transcendentals=0
        ),
        name="project_out",
    )(*blocks, w_output)


def body(
    row_size,
    col_size,
    hidden_in,
    norm_gain,
    w_query,
    key_weight,
    value_weight,
    w_output,
    stored_keys,
    stored_values,
    lengths,
):
    per_device = stored_keys.shape[0]
    capacity = stored_keys.shape[1]
    group_size = QUERY_HEADS // KEY_VALUE_HEADS
    head_size = HEAD_WIDTH
    kv_heads = stored_keys.shape[2] // head_size
    query_width = w_query.shape[1]
    kv_width = key_weight.shape[1]
    inputs = hidden_in.astype(jnp.float32)
    squares = jnp.sum(inputs * inputs, axis=1, keepdims=True)
    normed = (inputs * norm_gain[None, :]).astype(jnp.bfloat16)
    weights_all = jnp.concatenate([w_query, key_weight, value_weight], axis=1)
    partial_all = jnp.dot(normed, weights_all, preferred_element_type=jnp.float32)
    lanes = jnp.broadcast_to(squares, (squares.shape[0], head_size))
    projected = scatter_sum(jnp.concatenate([partial_all, lanes], axis=1), "row", row_size)
    my_scale = lax.rsqrt(projected[:, query_width + 2 * kv_width :][:, :1] / MODEL_WIDTH + 1e-05)
    query_part = projected[:, :query_width]
    key_part = projected[:, query_width : query_width + kv_width]
    value_part = projected[:, query_width + kv_width : query_width + 2 * kv_width]
    query_rotated_rows = apply_rotation(
        (query_part * my_scale).reshape(per_device, kv_heads * group_size, head_size), lengths
    )
    query_rotated_rows = query_rotated_rows.astype(jnp.bfloat16).reshape(
        per_device, kv_heads, group_size, head_size
    )
    key_rotated_rows = apply_rotation(
        (key_part * my_scale).reshape(per_device, kv_heads, head_size), lengths
    ).astype(jnp.bfloat16)
    value_request_rows = (
        (value_part * my_scale).reshape(per_device, kv_heads, head_size).astype(jnp.bfloat16)
    )
    every_key = stored_keys.reshape(per_device, capacity, kv_heads, head_size)
    every_value = stored_values.reshape(per_device, capacity, kv_heads, head_size)
    inverse = 1.0 / head_size**0.5
    score_new = (
        jnp.einsum(
            "rkgd,rkd->rkg",
            query_rotated_rows,
            key_rotated_rows,
            preferred_element_type=jnp.float32,
        )
        * inverse
    )
    tail_new = value_request_rows.astype(jnp.float32)[:, :, None, :]
    scores = (
        jnp.einsum(
            "rkgd,rckd->rkgc", query_rotated_rows, every_key, preferred_element_type=jnp.float32
        )
        * inverse
    )
    is_live = (jnp.arange(capacity, dtype=jnp.int32)[None, :] < lengths[:, None])[:, None, None, :]
    largest = jnp.maximum(jnp.max(jnp.where(is_live, scores, -jnp.inf), axis=-1), score_new)
    expo = jnp.where(is_live, jnp.exp(scores - largest[..., None]), 0.0)
    expo_new = jnp.exp(score_new - largest)
    denom = jnp.sum(expo, axis=-1) + expo_new
    probs = (expo / denom[..., None]).astype(jnp.bfloat16)
    prob_new = (expo_new / denom).astype(jnp.bfloat16)
    heads_out = jnp.einsum(
        "rkgc,rckd->rkgd", probs, every_value, preferred_element_type=jnp.float32
    )
    heads_out = heads_out + prob_new.astype(jnp.float32)[..., None] * tail_new
    heads_out = heads_out.astype(jnp.bfloat16).reshape(
        per_device, kv_heads * group_size * head_size
    )
    partial_out = jnp.dot(
        gather_rows(heads_out, "row", row_size),
        w_output,
        preferred_element_type=jnp.float32,
    )
    return scatter_sum(partial_out, "col", col_size).astype(jnp.bfloat16)


def direct_body(
    size,
    hidden_in,
    norm_gain,
    w_query,
    key_weight,
    value_weight,
    w_output,
    stored_keys,
    stored_values,
    lengths,
):
    head_size = HEAD_WIDTH
    parts = project_in(hidden_in, norm_gain, w_query, key_weight, value_weight)
    shares = [parts[0]] + [
        swap_with(parts[mask], "row", size, mask) for mask in partner_order(size)
    ]
    mine = attend(
        shares, lengths, stored_keys[0], stored_values[0], w_query.shape[1] // head_size
    )
    blocks = [mine] + [None] * (size - 1)
    for mask in partner_order(size):
        blocks[mask] = swap_with(mine, "row", size, mask)
    parts = project_out(blocks, w_output, size)
    received = [swap_with(parts[mask], "col", size, mask) for mask in partner_order(size)]
    total = parts[0]
    for part in received:
        total = total + part
    return total.astype(jnp.bfloat16)


def fits_direct(mesh):
    size = mesh.shape["row"]
    return is_direct(size) and size == mesh.shape["col"] == KEY_VALUE_HEADS == REQUEST_COUNT


def solution(mesh):
    placed = (
        P("rep", "row"),
        P("row"),
        P("row", "col"),
        P("row", "col"),
        P("row", "col"),
        P("col", "row"),
        P(("rep", "row"), None, "col"),
        P(("rep", "row"), None, "col"),
        P(("rep", "row")),
    )
    if fits_direct(mesh):
        sized = functools.partial(direct_body, mesh.shape["row"])
    else:
        sized = functools.partial(body, mesh.shape["row"], mesh.shape["col"])
    return jax.shard_map(
        sized, mesh=mesh, in_specs=placed, out_specs=P(("rep", "col"), "row"), check_vma=False
    )
```

```python
import functools

import jax
import jax.numpy as jnp
from jax import lax
from jax.experimental import pallas as pl
from jax.experimental.pallas import tpu as pltpu
from jax.sharding import PartitionSpec as P

MODEL_WIDTH = 16384
QUERY_HEADS = 64
KEY_VALUE_HEADS = 4
HEAD_WIDTH = 128
REQUEST_COUNT = 4


def apply_rotation(values, positions):
    half_dim = values.shape[-1] // 2
    head_size = values.shape[-1]
    frequency = 500000.0 ** (-(jnp.arange(half_dim, dtype=jnp.float32) * 2.0 / head_size))
    angles = positions.astype(jnp.float32)[:, None] * frequency[None, :]
    cosine = jnp.cos(angles)[:, None, :]
    sine_part = jnp.sin(angles)[:, None, :]
    first = values[..., :half_dim]
    second = values[..., half_dim:]
    return jnp.concatenate(
        [first * cosine - second * sine_part, second * cosine + first * sine_part], axis=-1
    )


DIRECT_LIMIT = 8
MIB = 1024 * 1024
VMEM_HELD = 26 * MIB
PRIORITY = 1
BLOCK = 1024
TAIL = 128


def is_direct(size):
    return 1 < size <= DIRECT_LIMIT and size & (size - 1) == 0


def partner_order(size):
    return range(size - 1, 0, -1)


def swap_with(values, axis, size, mask):
    return lax.ppermute(values, axis, [(i, i ^ mask) for i in range(size)])


def scatter_sum(values, axis, size):
    if not is_direct(size):
        return lax.psum_scatter(values, axis, scatter_dimension=0, tiled=True)
    share = values.shape[0] // size
    me = lax.axis_index(axis)
    total = lax.dynamic_slice_in_dim(values, me * share, share, 0)
    received = [
        swap_with(
            lax.dynamic_slice_in_dim(values, (me ^ mask) * share, share, 0), axis, size, mask
        )
        for mask in partner_order(size)
    ]
    for part in received:
        total = total + part
    return total


def gather_rows(values, axis, size):
    if not is_direct(size):
        return lax.all_gather(values, axis, axis=0, tiled=True)
    me = lax.axis_index(axis)
    blocks = [values] * size
    for mask in partner_order(size):
        blocks[mask] = swap_with(values, axis, size, mask)
    ordered = []
    for place in range(size):
        block = blocks[0]
        for mask in range(1, size):
            block = jnp.where((me ^ mask) == place, blocks[mask], block)
        ordered.append(block)
    return jnp.concatenate(ordered, axis=0)


def in_hbm(array):
    return pltpu.with_memory_space_constraint(array, pltpu.HBM)


def block_starts(depth):
    blocks = []
    start = 0
    while start < depth:
        size = min(BLOCK, depth - start)
        while size > TAIL and size * 2 > depth - start:
            size //= 2
        blocks.append((start, size))
        start += size
    return blocks


def project_kernel(row_size, blocks, hidden, gain, w_query, w_key, w_value, *refs):
    shares = refs[:row_size]
    inputs_near, gain_near, query_buffer, key_buffer, value_buffer, sems, left, total = refs[
        row_size:
    ]
    requests, depth = hidden.shape
    query_width, kv_width = w_query.shape[1], w_key.shape[1]
    first = [
        pltpu.make_async_copy(hidden, inputs_near, sems.at[0]),
        pltpu.make_async_copy(gain, gain_near, sems.at[1]),
    ]
    stages = [
        (pltpu.make_async_copy(w_key, key_buffer, sems.at[2]), 1, key_buffer, 0, depth),
        (pltpu.make_async_copy(w_value, value_buffer, sems.at[3]), 2, value_buffer, 0, depth),
    ]
    for step, (start, size) in enumerate(blocks):
        rows = pl.ds(start, size)
        copy = pltpu.make_async_copy(
            w_query.at[rows], query_buffer.at[rows], sems.at[4 + step]
        )
        stages.append((copy, 0, query_buffer, start, size))
    stages = stages[2:4] + stages[:2] + stages[4:]
    for copy in first:
        copy.start()
    for stage in stages:
        stage[0].start(priority=PRIORITY)
    for copy in first:
        copy.wait()
    inputs = inputs_near[...].astype(jnp.float32)
    left[...] = jnp.zeros_like(left)
    left[:requests, :] = inputs * gain_near[...]
    normed = left[...].astype(jnp.bfloat16)
    squares = jnp.sum(inputs * inputs, axis=1, keepdims=True)
    total[:requests, query_width + 2 * kv_width :] = jnp.broadcast_to(
        squares, (requests, HEAD_WIDTH)
    )
    sums = [None, None, None]
    for copy, which, near, start, size in stages:
        copy.wait()
        part = jnp.dot(
            normed[:, start : start + size],
            near[start : start + size, :],
            preferred_element_type=jnp.float32,
        )
        sums[which] = part if sums[which] is None else sums[which] + part
    total[:, query_width : query_width + kv_width] = sums[1]
    total[:, query_width + kv_width : query_width + 2 * kv_width] = sums[2]
    total[:, :query_width] = sums[0]
    here = lax.axis_index("row")
    for mask in range(row_size):
        shares[mask][...] = total[pl.ds(here ^ mask, 1), :]


def project_in(hidden_in, norm_gain, w_query, key_weight, value_weight):
    row_size = hidden_in.shape[0]
    depth, query_width = w_query.shape
    kv_width = key_weight.shape[1]
    blocks = block_starts(depth)
    width = query_width + 2 * kv_width + HEAD_WIDTH
    near = pl.BlockSpec(memory_space=pltpu.VMEM)
    far = pl.BlockSpec(memory_space=pltpu.HBM)
    size = 2 * depth * (query_width + 2 * kv_width)
    return pl.pallas_call(
        functools.partial(project_kernel, row_size, blocks),
        out_shape=[jax.ShapeDtypeStruct((1, width), jnp.float32)] * row_size,
        in_specs=[far] * 5,
        out_specs=[near] * row_size,
        scratch_shapes=[
            pltpu.VMEM((row_size, depth), jnp.bfloat16),
            pltpu.VMEM((1, depth), jnp.float32),
            pltpu.VMEM((depth, query_width), jnp.bfloat16),
            pltpu.VMEM((depth, kv_width), jnp.bfloat16),
            pltpu.VMEM((depth, kv_width), jnp.bfloat16),
            pltpu.SemaphoreType.DMA((4 + len(blocks),)),
            pltpu.VMEM((8, depth), jnp.float32),
            pltpu.VMEM((8, width), jnp.float32),
        ],
        compiler_params=pltpu.CompilerParams(vmem_limit_bytes=VMEM_HELD),
        cost_estimate=pl.CostEstimate(
            flops=row_size * size, bytes_accessed=size, transcendentals=0
        ),
        name="project_in",
    )(*map(in_hbm, (hidden_in, norm_gain.reshape(1, depth), w_query, key_weight, value_weight)))


def turn_kernel(ready, keys, turned):
    turned[...] = keys[...].T


def turn_keys(ready, keys):
    near = pl.BlockSpec(memory_space=pltpu.VMEM)
    return pl.pallas_call(
        turn_kernel,
        out_shape=jax.ShapeDtypeStruct(keys.shape[::-1], keys.dtype),
        in_specs=[near, near],
        out_specs=near,
        compiler_params=pltpu.CompilerParams(vmem_limit_bytes=4 * MIB),
        cost_estimate=pl.CostEstimate(
            flops=0, bytes_accessed=4 * keys.shape[0] * keys.shape[1], transcendentals=0
        ),
        name="turn_keys",
    )(ready, keys)


def attend_kernel(row_size, *refs):
    shares = refs[:row_size]
    length, cosine, sine, keys, values, heads, rows = refs[row_size:]
    heads_count, width = heads.shape
    summed = shares[0][...]
    for part in shares[1:]:
        summed = summed + part[...]
    query_width = heads_count * width
    squares = summed[:, query_width + 2 * width :]
    scale = lax.rsqrt(squares / MODEL_WIDTH + 1e-05)
    for head in range(heads_count):
        rows[head : head + 1, :] = summed[:, head * width : (head + 1) * width] * scale
    key_row = summed[:, query_width : query_width + width] * scale
    value_row = summed[:, query_width + width : query_width + 2 * width] * scale
    rows[heads_count : heads_count + 8, :] = jnp.broadcast_to(key_row, (8, width))
    both = rows[...]
    turned = both * cosine[...] + pltpu.roll(both, width // 2, 1) * sine[...]
    turned = turned.astype(jnp.bfloat16)
    query = turned[:heads_count]
    key_new = turned[heads_count : heads_count + 8].astype(jnp.float32)[:1]
    value_new = value_row.astype(jnp.bfloat16).astype(jnp.float32)
    inverse = 1.0 / width**0.5
    scores = (
        jnp.dot(query, keys[...], preferred_element_type=jnp.float32) * inverse
    )
    score_new = (
        jnp.sum(query.astype(jnp.float32) * key_new, axis=1, keepdims=True) * inverse
    )
    place = lax.broadcasted_iota(jnp.int32, scores.shape, 1)
    live = place < length[0]
    scores = jnp.where(live, scores, -jnp.inf)
    largest = jnp.maximum(jnp.max(scores, axis=1, keepdims=True), score_new)
    expo = jnp.exp(scores - largest)
    expo_new = jnp.exp(score_new - largest)
    part = 1.0 / (jnp.sum(expo, axis=1, keepdims=True) + expo_new)
    probs = (expo * part).astype(jnp.bfloat16)
    prob_new = (expo_new * part).astype(jnp.bfloat16).astype(jnp.float32)
    mixed = jnp.dot(probs, values[...], preferred_element_type=jnp.float32)
    heads[...] = (mixed + prob_new * value_new).astype(jnp.bfloat16)


def attend(shares, lengths, keys, values, heads_count):
    row_size = len(shares)
    width, slots = keys.shape
    half = width // 2
    frequency = 500000.0 ** (-(jnp.arange(half, dtype=jnp.float32) * 2.0 / width))
    angles = lengths.astype(jnp.float32)[:, None] * frequency[None, :]
    cosine, sine = jnp.cos(angles), jnp.sin(angles)
    cosine = jnp.concatenate([cosine, cosine], axis=1)
    sine = jnp.concatenate([-sine, sine], axis=1)
    near = pl.BlockSpec(memory_space=pltpu.VMEM)
    return pl.pallas_call(
        functools.partial(attend_kernel, row_size),
        out_shape=jax.ShapeDtypeStruct((heads_count, width), jnp.bfloat16),
        in_specs=[near] * row_size + [pl.BlockSpec(memory_space=pltpu.SMEM)] + [near] * 4,
        out_specs=near,
        scratch_shapes=[pltpu.VMEM((heads_count + 8, width), jnp.float32)],
        compiler_params=pltpu.CompilerParams(vmem_limit_bytes=4 * MIB),
        cost_estimate=pl.CostEstimate(
            flops=4 * heads_count * slots * width,
            bytes_accessed=4 * slots * width,
            transcendentals=heads_count * slots,
        ),
        name="attend",
    )(*shares, lengths, cosine, sine, keys, values)


def output_kernel(row_size, col_size, chunk, *refs):
    heads = refs[:row_size]
    weight = refs[row_size]
    shares = refs[row_size + 1 : row_size + 1 + col_size]
    left, total = refs[row_size + 1 + col_size :]
    count = heads[0].shape[0]
    width = heads[0].shape[1]
    left[...] = jnp.zeros_like(left)
    for slot in range(row_size):
        rows = heads[slot][...].astype(jnp.float32)
        for head in range(count):
            left[slot : slot + 1, head * width : (head + 1) * width] = rows[head : head + 1, :]
    lhs = left[...].astype(jnp.bfloat16)
    for start in range(0, weight.shape[1], chunk):
        total[:, start : start + chunk] = jnp.dot(
            lhs, weight[:, start : start + chunk], preferred_element_type=jnp.float32
        )
    here = lax.axis_index("row")
    lane = lax.axis_index("col")
    for mask in range(col_size):
        row = total[pl.ds((lane ^ mask) ^ here, 1), :]
        piece = shares[mask].shape[1]
        for part in range(8):
            shares[mask][part : part + 1, :] = row[:, part * piece : (part + 1) * piece]


def project_out(blocks, w_output, col_size):
    row_size = len(blocks)
    depth, width = w_output.shape
    whole = pl.BlockSpec(memory_space=pltpu.VMEM)
    return pl.pallas_call(
        functools.partial(output_kernel, row_size, col_size, min(width, 512)),
        out_shape=[jax.ShapeDtypeStruct((8, width // 8), jnp.float32)] * col_size,
        in_specs=[whole] * (row_size + 1),
        out_specs=[whole] * col_size,
        scratch_shapes=[
            pltpu.VMEM((8, depth), jnp.float32),
            pltpu.VMEM((8, width), jnp.float32),
        ],
        compiler_params=pltpu.CompilerParams(vmem_limit_bytes=4 * MIB),
        cost_estimate=pl.CostEstimate(
            flops=2 * row_size * depth * width, bytes_accessed=2 * depth * width, transcendentals=0
        ),
        name="project_out",
    )(*blocks, w_output)


def sum_kernel(*refs):
    parts = refs[:-1]
    total = parts[0][...]
    for part in parts[1:]:
        total = total + part[...]
    piece = total.shape[1]
    for part in range(8):
        refs[-1][:, part * piece : (part + 1) * piece] = total[part : part + 1, :].astype(
            refs[-1].dtype
        )


def sum_rows(parts):
    near = pl.BlockSpec(memory_space=pltpu.VMEM)
    return pl.pallas_call(
        sum_kernel,
        out_shape=jax.ShapeDtypeStruct((1, parts[0].size), jnp.bfloat16),
        in_specs=[near] * len(parts),
        out_specs=near,
        compiler_params=pltpu.CompilerParams(vmem_limit_bytes=4 * MIB),
        name="sum_rows",
    )(*parts)


def body(
    row_size,
    col_size,
    hidden_in,
    norm_gain,
    w_query,
    key_weight,
    value_weight,
    w_output,
    stored_keys,
    stored_values,
    lengths,
):
    per_device = stored_keys.shape[0]
    capacity = stored_keys.shape[1]
    group_size = QUERY_HEADS // KEY_VALUE_HEADS
    head_size = HEAD_WIDTH
    kv_heads = stored_keys.shape[2] // head_size
    query_width = w_query.shape[1]
    kv_width = key_weight.shape[1]
    inputs = hidden_in.astype(jnp.float32)
    squares = jnp.sum(inputs * inputs, axis=1, keepdims=True)
    normed = (inputs * norm_gain[None, :]).astype(jnp.bfloat16)
    weights_all = jnp.concatenate([w_query, key_weight, value_weight], axis=1)
    partial_all = jnp.dot(normed, weights_all, preferred_element_type=jnp.float32)
    lanes = jnp.broadcast_to(squares, (squares.shape[0], head_size))
    projected = scatter_sum(jnp.concatenate([partial_all, lanes], axis=1), "row", row_size)
    my_scale = lax.rsqrt(projected[:, query_width + 2 * kv_width :][:, :1] / MODEL_WIDTH + 1e-05)
    query_part = projected[:, :query_width]
    key_part = projected[:, query_width : query_width + kv_width]
    value_part = projected[:, query_width + kv_width : query_width + 2 * kv_width]
    query_rotated_rows = apply_rotation(
        (query_part * my_scale).reshape(per_device, kv_heads * group_size, head_size), lengths
    )
    query_rotated_rows = query_rotated_rows.astype(jnp.bfloat16).reshape(
        per_device, kv_heads, group_size, head_size
    )
    key_rotated_rows = apply_rotation(
        (key_part * my_scale).reshape(per_device, kv_heads, head_size), lengths
    ).astype(jnp.bfloat16)
    value_request_rows = (
        (value_part * my_scale).reshape(per_device, kv_heads, head_size).astype(jnp.bfloat16)
    )
    every_key = stored_keys.reshape(per_device, capacity, kv_heads, head_size)
    every_value = stored_values.reshape(per_device, capacity, kv_heads, head_size)
    inverse = 1.0 / head_size**0.5
    score_new = (
        jnp.einsum(
            "rkgd,rkd->rkg",
            query_rotated_rows,
            key_rotated_rows,
            preferred_element_type=jnp.float32,
        )
        * inverse
    )
    tail_new = value_request_rows.astype(jnp.float32)[:, :, None, :]
    scores = (
        jnp.einsum(
            "rkgd,rckd->rkgc", query_rotated_rows, every_key, preferred_element_type=jnp.float32
        )
        * inverse
    )
    is_live = (jnp.arange(capacity, dtype=jnp.int32)[None, :] < lengths[:, None])[:, None, None, :]
    largest = jnp.maximum(jnp.max(jnp.where(is_live, scores, -jnp.inf), axis=-1), score_new)
    expo = jnp.where(is_live, jnp.exp(scores - largest[..., None]), 0.0)
    expo_new = jnp.exp(score_new - largest)
    denom = jnp.sum(expo, axis=-1) + expo_new
    probs = (expo / denom[..., None]).astype(jnp.bfloat16)
    prob_new = (expo_new / denom).astype(jnp.bfloat16)
    heads_out = jnp.einsum(
        "rkgc,rckd->rkgd", probs, every_value, preferred_element_type=jnp.float32
    )
    heads_out = heads_out + prob_new.astype(jnp.float32)[..., None] * tail_new
    heads_out = heads_out.astype(jnp.bfloat16).reshape(
        per_device, kv_heads * group_size * head_size
    )
    partial_out = jnp.dot(
        gather_rows(heads_out, "row", row_size),
        w_output,
        preferred_element_type=jnp.float32,
    )
    return scatter_sum(partial_out, "col", col_size).astype(jnp.bfloat16)


def direct_body(
    size,
    hidden_in,
    norm_gain,
    w_query,
    key_weight,
    value_weight,
    w_output,
    stored_keys,
    stored_values,
    lengths,
):
    head_size = HEAD_WIDTH
    parts = project_in(hidden_in, norm_gain, w_query, key_weight, value_weight)
    shares = [parts[0]] + [
        swap_with(parts[mask], "row", size, mask) for mask in partner_order(size)
    ]
    keys = turn_keys(parts[0], stored_keys[0])
    mine = attend(shares, lengths, keys, stored_values[0], w_query.shape[1] // head_size)
    blocks = [mine] + [None] * (size - 1)
    for mask in partner_order(size):
        blocks[mask] = swap_with(mine, "row", size, mask)
    parts = project_out(blocks, w_output, size)
    received = [swap_with(parts[mask], "col", size, mask) for mask in partner_order(size)]
    return sum_rows([parts[0]] + received)


def fits_direct(mesh):
    size = mesh.shape["row"]
    return is_direct(size) and size == mesh.shape["col"] == KEY_VALUE_HEADS == REQUEST_COUNT


def solution(mesh):
    placed = (
        P("rep", "row"),
        P("row"),
        P("row", "col"),
        P("row", "col"),
        P("row", "col"),
        P("col", "row"),
        P(("rep", "row"), None, "col"),
        P(("rep", "row"), None, "col"),
        P(("rep", "row")),
    )
    if fits_direct(mesh):
        sized = functools.partial(direct_body, mesh.shape["row"])
    else:
        sized = functools.partial(body, mesh.shape["row"], mesh.shape["col"])
    return jax.shard_map(
        sized, mesh=mesh, in_specs=placed, out_specs=P(("rep", "col"), "row"), check_vma=False
    )
```
